256 devices in a mesh: ctx: 128 (over x_lo, z, y, core), head: 2 (over x_hi).
Axes of the slice: x: 4 (x_hi: 2, x_lo: 2; x = x_hi * 2 + x_lo), y: 4, z: 8, core: 2. Of those that a mesh axis runs over, the one named last changes fastest.
Arguments:
- queries: bfloat16 [64, 32768, 128], P(None, ('ctx', 'head')), may hold values from -6 to 6
- keys: bfloat16 [8, 32768, 128], P(None, ('ctx', 'head')), may hold values from -6 to 6
- values: bfloat16 [8, 32768, 128], P(None, ('ctx', 'head')), may hold values from -6 to 6
- delta: bfloat16 [64, 32768], P(None, ('ctx', 'head')), may hold values from -270 to 270
- grad_out: bfloat16 [64, 32768, 128], P(None, ('ctx', 'head')), may hold values from -24 to 24
- lse: bfloat16 [64, 32768], P(None, ('ctx', 'head')), may hold values from 6 to 8
Outputs:
- query_grads: bfloat16 [64, 32768, 128], P(None, ('ctx', 'head'))
- key_grads: bfloat16 [8, 32768, 128], P(None, ('ctx', 'head'))
- value_grads: bfloat16 [8, 32768, 128], P(None, ('ctx', 'head'))
The draws below stay inside these ranges and needn't reach their ends.
All inputs are finite; a program needn't handle non-finite values.
Results may differ from the reference program's by a relative error of at most 0.005.
Values may be sent and summed in bfloat16 or wider, within the bound.
No kernel may reach another device: no remote copies, remote signals or barrier semaphores. Data moves between devices by JAX's collectives and lax.ppermute only.
A program may use at most 128 MiB of HBM per device.

```python
import math
import jax
import jax.numpy as jnp
from jax import lax

HEADS = 64
KV_HEADS = 8
HEAD_DIM = 128
BLOCK = 256
TOKENS = 32768
N_CTX = 128


def level_of(stream_key, shape, pieces, low, top_value):
    def one(dim, shards_of):
        draws = jax.random.uniform(jax.random.fold_in(jax.random.fold_in(stream_key, 6), dim), (shards_of,), jnp.float32, low / len(pieces), top_value / len(pieces))
        return jnp.repeat(jnp.exp(draws), shape[dim] // shards_of).reshape((-1,) + (1,) * (len(shape) - dim - 1))

    level = one(*pieces[0])
    for cut in pieces[1:]:
        level = level * one(*cut)
    return level


def bell_draw(rng, dims, deviation, most, shards=(), kind=jnp.bfloat16):
    values = deviation * jax.random.normal(rng, dims, jnp.float32)
    if shards:
        values = values * level_of(rng, dims, shards, -0.22, 0.18)
    return jnp.clip(values, -most, most).astype(kind)


def setup_inputs(seed: int = 0) -> dict:
    arg_keys = jax.random.split(jax.random.key(seed), 7)
    return {
        "queries": bell_draw(arg_keys[0], (HEADS, TOKENS, HEAD_DIM), 1.0, 6.0, ((1, 256),)),
        "keys": bell_draw(arg_keys[1], (KV_HEADS, TOKENS, HEAD_DIM), 1.0, 6.0, ((1, 256),)),
        "values": bell_draw(arg_keys[2], (KV_HEADS, TOKENS, HEAD_DIM), 1.0, 6.0, ((1, 256),)),
        "delta": bell_draw(arg_keys[3], (HEADS, TOKENS), (4.0 * HEAD_DIM ** 0.5), 270.0, ((1, 256),)),
        "grad_out": bell_draw(arg_keys[4], (HEADS, TOKENS, HEAD_DIM), 4.0, 24.0, ((1, 256),)),
        "lse": jnp.clip(6.0 + 2.0 * jax.random.uniform(arg_keys[5], (HEADS, TOKENS), jnp.float32) ** level_of(arg_keys[5], (HEADS, TOKENS), ((1, 256),), -0.2, 0.2), 6.0, 8.0).astype(jnp.bfloat16),
    }


def tile_grads(queries, delta, grads_out, lse, keys, values, allowed):
    heads, rows, width = queries.shape
    groups = keys.shape[0]
    ratio = heads // groups
    scale = 1.0 / math.sqrt(width)
    q_four = queries.astype(jnp.float32).reshape(groups, ratio, rows, width)
    g_four = grads_out.astype(jnp.float32).reshape(groups, ratio, rows, width)
    delta_f = delta.astype(jnp.float32).reshape(groups, ratio, rows)
    key_f = keys.astype(jnp.float32)
    val_f = values.astype(jnp.float32)
    scores = jnp.einsum('kgrd,kjd->kgrj', q_four, key_f) * scale
    probs = jnp.exp(scores - lse.astype(jnp.float32).reshape(groups, ratio, rows)[..., None])
    if allowed is not None:
        probs = jnp.where(allowed, probs, 0.0)
    probs_half = probs.astype(jnp.bfloat16).astype(jnp.float32)
    dvalue = jnp.einsum('kgrj,kgrd->kjd', probs_half, g_four)
    dprobs = jnp.einsum('kgrd,kjd->kgrj', g_four, val_f)
    dscores = (probs * (dprobs - delta_f[..., None])).astype(jnp.bfloat16).astype(jnp.float32)
    dquery = jnp.einsum('kgrj,kjd->kgrd', dscores, key_f) * scale
    dkey = jnp.einsum('kgrj,kgrd->kjd', dscores, q_four) * scale
    return (dquery.reshape(heads, rows, width), dkey, dvalue)

def reference(queries, keys, values, delta, grad_out, lse):
    blocks = N_CTX
    offset = blocks // 2
    span = BLOCK
    positions = jnp.arange(span, dtype=jnp.int32)
    causal = positions[None, :] <= positions[:, None]

    def take(array, index):
        return lax.dynamic_slice_in_dim(array, (index * span).astype(jnp.int32), span, 1)

    def one_block(index):
        far = jnp.maximum(index - offset, 0).astype(jnp.int32)
        q_blk = take(queries, index)
        d_blk = take(delta, index)
        g_blk = take(grad_out, index)
        l_blk = take(lse, index)
        dq_near, dk_near, dv_near = tile_grads(q_blk, d_blk, g_blk, l_blk, take(keys, index), take(values, index), causal)
        dq_far, dk_far, dv_far = tile_grads(q_blk, d_blk, g_blk, l_blk, take(keys, far), take(values, far), None)
        valid = (index >= offset).astype(jnp.float32)
        dq_blk = (dq_near + valid * dq_far).astype(jnp.bfloat16)
        return (dq_blk, dk_near, dv_near, valid * dk_far, valid * dv_far)
    dq_all, dk_near, dv_near, dk_far, dv_far = lax.map(one_block, jnp.arange(blocks, dtype=jnp.int32))
    dk_total = dk_near + jnp.concatenate([dk_far[offset:], jnp.zeros_like(dk_far[:blocks - offset])], 0)
    dv_total = dv_near + jnp.concatenate([dv_far[offset:], jnp.zeros_like(dv_far[:blocks - offset])], 0)

    def unblock(array):
        return jnp.transpose(array, (1, 0, 2, 3)).reshape(array.shape[1], blocks * span, array.shape[3])
    query_grads = unblock(dq_all)
    key_grads = unblock(dk_total.astype(jnp.bfloat16))
    value_grads = unblock(dv_total.astype(jnp.bfloat16))
    return (query_grads, key_grads, value_grads)
```

```python
import functools
import math

import jax
import jax.numpy as jnp
from jax import lax
from jax.experimental import pallas as pl
from jax.experimental.pallas import tpu as pltpu
from jax.sharding import PartitionSpec as P

LOG2E = math.log2(math.e)
NN = (((1,), (0,)), ((), ()))
NT = (((1,), (1,)), ((), ()))
TN = (((0,), (0,)), ((), ()))
AXES = ("ctx", "head")


def dot(a, b, dims):
    return lax.dot_general(a, b, dims, preferred_element_type=jnp.float32)


def route(x, pairs):
    far = lax.axis_size("ctx") // 2

    def device(role, c):
        return (c + (far if role[0] == "L" else 0)) * 2 + int(role[1])

    table = []
    for pair in pairs.split():
        src, dst = pair.split(">")
        table += [(device(src, c), device(dst, c)) for c in range(far)]
    return lax.ppermute(x, AXES, table)


def head_tiles(q_ref, g_ref, lse, delta, g, ratio):
    rows = q_ref.shape[1]
    lo = g * ratio
    width = q_ref.shape[2]
    q = q_ref[lo : lo + ratio].reshape(ratio * rows, width)
    g_out = g_ref[lo : lo + ratio].reshape(ratio * rows, width)
    lse_row = jnp.concatenate([lse[lo + i : lo + i + 1, :] for i in range(ratio)], 1)
    delta_row = jnp.concatenate([delta[lo + i : lo + i + 1, :] for i in range(ratio)], 1)
    return q, g_out, lse_row, delta_row


def grads(q, g_out, lse_row, delta_row, k, v, causal, rows):
    scale = 1.0 / math.sqrt(q.shape[1])
    probs = jnp.exp2(dot(k, q, NT) * (scale * LOG2E) - lse_row)
    if causal:
        key = lax.broadcasted_iota(jnp.int32, probs.shape, 0)
        row = lax.broadcasted_iota(jnp.int32, probs.shape, 1) % rows
        probs = jnp.where(key <= row, probs, 0.0)
    dprobs = dot(v, g_out, NT)
    dscores = (probs * (dprobs - delta_row)).astype(jnp.bfloat16)
    dvalue = dot(probs.astype(jnp.bfloat16), g_out, NN)
    dkey = dot(dscores, q, NN) * scale
    dquery = dot(dscores, k, TN) * scale
    return dquery, dkey, dvalue


def unit_kernel(causal, flag_at, ratio, flags, *refs):
    q_ref, g_ref, lse_ref, delta_ref = refs[:4]
    refs = refs[4:]
    dq_in = None
    if flag_at is not None:
        dq_in, refs = refs[0], refs[1:]
    n = (len(refs) - 1) // 2
    kv_refs, dq_ref, out_refs = refs[:n], refs[n], refs[n + 1 :]
    rows, width = q_ref.shape[1:]
    groups = q_ref.shape[0] // ratio

    def work():
        lse = lse_ref[...].astype(jnp.float32) * LOG2E
        delta = delta_ref[...].astype(jnp.float32)
        for g in range(groups):
            q, g_out, lse_row, delta_row = head_tiles(q_ref, g_ref, lse, delta, g, ratio)
            k = jnp.concatenate([r[0, g] for r in kv_refs], 0)
            v = jnp.concatenate([r[1, g] for r in kv_refs], 0)
            dq, dk, dv = grads(q, g_out, lse_row, delta_row, k, v, causal, rows)
            dq = dq.reshape(ratio, rows, width)
            at = slice(g * ratio, (g + 1) * ratio)
            if dq_in is not None:
                dq = dq + dq_in[at]
            dq_ref[at] = dq.astype(dq_ref.dtype)
            for i, out in enumerate(out_refs):
                cut = slice(i * rows, (i + 1) * rows)
                out[0, g] = dk[cut].astype(out.dtype)
                out[1, g] = dv[cut].astype(out.dtype)

    if flag_at is None:
        work()
    else:
        pl.when(flags[flag_at] == 1)(work)

        @pl.when(flags[flag_at] == 0)
        def _():
            dq_ref[...] = dq_in[...].astype(dq_ref.dtype)


def unit_call(name, flags, q, g_out, lse, delta, dq_in, kvs, *, causal, flag_at, dq_dtype, kv_dtype,
              first=0, dq_alias=None, step=2):
    heads, rows, width = q.shape
    groups = kvs[0].shape[1]
    all_groups = 8 * heads // 64
    ratio = heads // all_groups
    off = first // step
    heads_block = pl.BlockSpec((step * ratio, rows, width), lambda i, f: (i + off, 0, 0))
    rows_block = pl.BlockSpec((step * ratio, rows), lambda i, f: (i + off, 0))
    kv_block = pl.BlockSpec((2, step, rows, width), lambda i, f: (0, i, 0, 0))
    args = [q, g_out, lse, delta]
    in_specs = [heads_block, heads_block, rows_block, rows_block]
    if dq_in is not None:
        args.append(dq_in)
        in_specs.append(heads_block)
    args += kvs
    in_specs += [kv_block] * len(kvs)
    aliases = {}
    kernel = functools.partial(unit_kernel, causal, flag_at, ratio)
    if dq_alias is not None:
        aliases = {len(args) + 1: 0}
        args.append(dq_alias)
        in_specs.append(pl.BlockSpec(memory_space=pl.ANY))
        inner, drop = kernel, len(args)

        def kernel(flags, *refs):
            inner(flags, *refs[: drop - 1], *refs[drop:])

    pairs = len(kvs) * groups * ratio * rows * rows
    return pl.pallas_call(
        kernel,
        grid_spec=pltpu.PrefetchScalarGridSpec(
            num_scalar_prefetch=1,
            grid=(groups // step,),
            in_specs=in_specs,
            out_specs=[heads_block] + [kv_block] * len(kvs),
        ),
        out_shape=[jax.ShapeDtypeStruct(q.shape, dq_dtype)]
        + [jax.ShapeDtypeStruct(kvs[0].shape, kv_dtype)] * len(kvs),
        input_output_aliases=aliases,
        compiler_params=pltpu.CompilerParams(vmem_limit_bytes=40 << 20),
        cost_estimate=pl.CostEstimate(
            flops=10 * pairs * width, bytes_accessed=8 << 20, transcendentals=pairs
        ),
        name=name,
    )(flags, *args)


def local(queries, keys, values, delta, grad_out, lse):
    half = lax.axis_index("head")
    is_late = lax.axis_index("ctx") >= lax.axis_size("ctx") // 2
    flags = jnp.stack([half.astype(jnp.int32), is_late.astype(jnp.int32)])
    kv = jnp.stack([keys, values])
    kv_z = route(kv, "E0>E1 L0>L1")
    kv_x = route(kv, "E0>L0 E1>L1")
    kv_y = route(kv, "E0>L1 E1>L0")
    call = functools.partial(unit_call, flags=flags, q=queries, g_out=grad_out, lse=lse, delta=delta)
    dq, dkv = call("diag", dq_in=None, kvs=[kv], causal=True, flag_at=None,
                   dq_dtype=jnp.float32, kv_dtype=jnp.float32)
    dq, dz = call("near", dq_in=dq, kvs=[kv_z], causal=False, flag_at=0,
                  dq_dtype=jnp.float32, kv_dtype=jnp.bfloat16)
    rz = route(dz, "E1>E0 L1>L0")
    dq, dx, dy = call("far", dq_in=dq, kvs=[kv_x, kv_y], causal=False, flag_at=1,
                      dq_dtype=jnp.bfloat16, kv_dtype=jnp.bfloat16)
    rx = route(dx, "L0>E0 L1>E1")
    ry = route(dy, "L1>E0 L0>E1")
    f32 = jnp.float32
    total = dkv + rz.astype(f32) + (rx.astype(f32) + ry.astype(f32))
    total = total.astype(jnp.bfloat16)
    return dq, total[0], total[1]


def solution(mesh):
    spec3 = P(None, AXES, None)
    spec2 = P(None, AXES)
    return jax.shard_map(
        local,
        mesh=mesh,
        in_specs=(spec3, spec3, spec3, spec2, spec3, spec2),
        out_specs=(spec3, spec3, spec3),
        check_vma=False,
    )
```

```python
import functools
import math

import jax
import jax.numpy as jnp
from jax import lax
from jax.experimental import pallas as pl
from jax.experimental.pallas import tpu as pltpu
from jax.sharding import PartitionSpec as P

LOG2E = math.log2(math.e)
NN = (((1,), (0,)), ((), ()))
NT = (((1,), (1,)), ((), ()))
TN = (((0,), (0,)), ((), ()))
AXES = ("ctx", "head")
F32 = jnp.float32
BF16 = jnp.bfloat16
VMEM = pl.BlockSpec(memory_space=pltpu.VMEM)
SMEM = pl.BlockSpec(memory_space=pltpu.SMEM)
HBM = pl.BlockSpec(memory_space=pltpu.HBM)
CHUNKS = 2


def dot(a, b, dims):
    return lax.dot_general(a, b, dims, preferred_element_type=F32)


def route(x, pairs):
    far = lax.axis_size("ctx") // 2

    def device(role, c):
        return (c + (far if role[0] == "L" else 0)) * 2 + int(role[1])

    table = []
    for pair in pairs.split():
        src, dst = pair.split(">")
        table += [(device(src, c), device(dst, c)) for c in range(far)]
    return lax.ppermute(x, AXES, table)


def call(kernel, name, in_specs, out_specs, out_shape, scratch=(), aliases=None):
    return pl.pallas_call(
        kernel,
        in_specs=in_specs,
        out_specs=out_specs,
        out_shape=out_shape,
        scratch_shapes=list(scratch),
        input_output_aliases=aliases or {},
        compiler_params=pltpu.CompilerParams(vmem_limit_bytes=24 << 20),
        cost_estimate=pl.CostEstimate(flops=1, bytes_accessed=1 << 20, transcendentals=0),
        name=name,
    )


def group_grads(q_ref, g_ref, lse_ref, delta_ref, g, kvs, at, causal):
    rows, width = q_ref.shape[1:]
    ratio = 8
    lo = g * ratio
    scale = 1.0 / math.sqrt(width)
    q = q_ref[lo : lo + ratio].reshape(ratio * rows, width)
    g_out = g_ref[lo : lo + ratio].reshape(ratio * rows, width)
    base = lo // 16 * 16
    lse = lse_ref[base : base + 16].astype(F32)[lo - base : lo - base + ratio] * LOG2E
    delta = delta_ref[base : base + 16].astype(F32)[lo - base : lo - base + ratio]
    lse_row = jnp.concatenate([lse[i : i + 1, :] for i in range(ratio)], 1)
    delta_row = jnp.concatenate([delta[i : i + 1, :] for i in range(ratio)], 1)
    k = jnp.concatenate([r[0, at] for r in kvs], 0)
    v = jnp.concatenate([r[1, at] for r in kvs], 0)
    probs = jnp.exp2(dot(k, q, NT) * (scale * LOG2E) - lse_row)
    if causal:
        key = lax.broadcasted_iota(jnp.int32, probs.shape, 0)
        row = lax.broadcasted_iota(jnp.int32, probs.shape, 1) % rows
        probs = jnp.where(key <= row, probs, 0.0)
    dprobs = dot(v, g_out, NT)
    dscores = (probs * (dprobs - delta_row)).astype(BF16)
    dvalue = dot(probs.astype(BF16), g_out, NN)
    dkey = dot(dscores, q, NN) * scale
    dquery = dot(dscores, k, TN) * scale
    return dquery.reshape(ratio, rows, width), dkey, dvalue


def pack_kernel(flags, k_ref, v_ref, *refs):
    outs, sem = refs[:-1], refs[-1]
    copies = []
    for i, out in enumerate(outs):
        n = out.shape[1]
        for j, src in enumerate((k_ref, v_ref)):
            copies.append(pltpu.make_async_copy(src.at[pl.ds(i * n, n)], out.at[j], sem.at[2 * i + j]))
    for c in copies:
        c.start()
    for c in copies:
        c.wait()


def repeat(held, later):
    for src, out in zip(held, later):
        out[...] = src[...]


def load_kernel(q_hbm, g_hbm, lse_hbm, delta_hbm, *refs):
    n = (len(refs) - 5) // 2
    held, (q_ref, g_ref, lse_ref, delta_ref), later, sem = (
        refs[:n], refs[n : n + 4], refs[n + 4 : -1], refs[-1]
    )
    copies = [
        pltpu.make_async_copy(lse_hbm, lse_ref, sem.at[0]),
        pltpu.make_async_copy(delta_hbm, delta_ref, sem.at[1]),
    ]
    pieces = 4
    size = q_hbm.shape[0] // pieces
    for i in range(pieces):
        cut = pl.ds(i * size, size)
        copies.append(pltpu.make_async_copy(q_hbm.at[cut], q_ref.at[cut], sem.at[2 + 2 * i]))
        copies.append(pltpu.make_async_copy(g_hbm.at[cut], g_ref.at[cut], sem.at[3 + 2 * i]))
    for c in copies:
        c.start()
    repeat(held, later)
    for c in copies:
        c.wait()


def pair_kernel(first, flag_at, n_kv, n_held, n_after, with_sum, flags, q_ref, g_ref, lse_ref, delta_ref, *refs):
    refs = refs[n_after:]
    if with_sum:
        rx_ref, ry_ref, rz_ref, *refs = refs
        *refs, sum_ref = refs
        sum_ref[...] = rx_ref[...].astype(F32) + ry_ref[...].astype(F32) + rz_ref[...].astype(F32)
    kv_refs, refs = refs[:n_kv], refs[n_kv:]
    held, refs = refs[:n_held], refs[n_held:]
    dq_ref, outs, later = refs[0], refs[1 : 1 + n_kv], refs[1 + n_kv :]
    repeat(held, later)
    groups = kv_refs[0].shape[1]
    rows = q_ref.shape[1]
    ratio = 8

    @pl.when(flags[flag_at] == 1)
    def _():
        for i in range(groups):
            dq, dk, dv = group_grads(
                q_ref, g_ref, lse_ref, delta_ref, first + i, kv_refs, i, False
            )
            dq_ref[i * ratio : (i + 1) * ratio] = dq
            for j, out in enumerate(outs):
                out[0, i] = dk[j * rows : (j + 1) * rows].astype(BF16)
                out[1, i] = dv[j * rows : (j + 1) * rows].astype(BF16)


def diag_kernel(flags, q_ref, g_ref, lse_ref, delta_ref, *refs):
    parts, near_refs, far_refs = refs[0:2], refs[2:4], refs[4:6]
    dq_hbm, dkv_ref, dq_half, sem = refs[6:]
    n = parts[0].shape[1]
    ratio = 8
    stores = []
    has_near, has_far = flags[0] == 1, flags[1] == 1
    for g in range(2 * n):
        c, i = g // n, g % n
        dq, dk, dv = group_grads(q_ref, g_ref, lse_ref, delta_ref, g, [parts[c]], i, True)
        at = slice(g * ratio, (g + 1) * ratio)
        of = slice(i * ratio, (i + 1) * ratio)
        dq = dq + jnp.where(has_near, near_refs[c][of], 0.0)
        dq = dq + jnp.where(has_far, far_refs[c][of], 0.0)
        dq_half[at] = dq.astype(BF16)
        cut = pl.ds(g * ratio, ratio)
        stores.append(pltpu.make_async_copy(dq_half.at[cut], dq_hbm.at[cut], sem.at[g]))
        stores[-1].start()
        dkv_ref[0, g] = dk
        dkv_ref[1, g] = dv
    for c in stores:
        c.wait()


def final_kernel(dkv_ref, sum_ref, rx_ref, ry_ref, rz_ref, dk_hbm, dv_hbm, half, sem):
    n = rz_ref.shape[1]
    copies = []
    for j, out in enumerate((dk_hbm, dv_hbm)):
        half[j, :n] = (dkv_ref[j, :n] + sum_ref[j]).astype(BF16)
        far = rx_ref[j].astype(F32) + ry_ref[j].astype(F32)
        half[j, n:] = (dkv_ref[j, n:] + rz_ref[j].astype(F32) + far).astype(BF16)
        copies.append(pltpu.make_async_copy(half.at[j], out, sem.at[j]))
        copies[-1].start()
    for c in copies:
        c.wait()


def in_hbm(x):
    return pltpu.with_memory_space_constraint(x, pltpu.HBM)


def local(queries, keys, values, delta, grad_out, lse):
    half = lax.axis_index("head")
    is_late = lax.axis_index("ctx") >= lax.axis_size("ctx") // 2
    flags = jnp.stack([half.astype(jnp.int32), is_late.astype(jnp.int32)])
    heads, rows, width = queries.shape
    groups = keys.shape[0]
    n = groups // CHUNKS
    shape = jax.ShapeDtypeStruct
    part = shape((2, n, rows, width), BF16)
    dq_part = shape((heads // CHUNKS, rows, width), F32)
    sem = pltpu.SemaphoreType.DMA
    parts = call(
        pack_kernel, "pack", [SMEM] + [HBM] * 2, [VMEM] * CHUNKS, [part] * CHUNKS, [sem((2 * CHUNKS,))]
    )(flags, in_hbm(keys), in_hbm(values))

    up0, down0 = route(parts[0], "E0>L0 E1>L1 L0>E0"), route(parts[0], "E0>L1 E1>L0")
    *rows_in, later = call(
        load_kernel,
        "load",
        [HBM] * 4 + [VMEM],
        [VMEM] * 5,
        [shape(x.shape, BF16) for x in (queries, grad_out, lse, delta)] + [part],
        [sem((10,))],
    )(*(in_hbm(x) for x in (queries, grad_out, lse, delta)), parts[1])
    up1, down1 = route(later, "E0>L0 E1>L1 L0>E0"), route(later, "E0>L1 E1>L0")

    def to_second(x):
        return route(x, "E0>L1 L0>E1")

    def to_early(x, y):
        return route(x, "L0>E0 L1>E1"), route(y, "L1>E0 L0>E1")

    def pairs(name, flag_at, kvs, held=(), add=(), after=()):
        n_held, n_sum = len(held), len(add) // 3
        return call(
            functools.partial(
                pair_kernel, int(name[-1]) * n, flag_at, len(kvs), n_held, len(after), n_sum
            ),
            name,
            [SMEM] + [VMEM] * (4 + len(after) + len(kvs) + n_held + len(add)),
            [VMEM] * (1 + len(kvs) + n_held + n_sum),
            [dq_part] + [part] * (len(kvs) + n_held) + [shape(part.shape, F32)] * n_sum,
        )(flags, *rows_in, *after, *add, *kvs, *held)

    kv_near0 = to_second(up0)
    dq_far0, dx0, dy0 = pairs("far0", 1, [up0, down0])
    rx0, ry0 = to_early(dx0, dy0)
    dq_near0, dz0, mid1 = pairs("near0", 0, [kv_near0], held=[up1], after=[dq_far0])
    rz0 = route(dz0, "E1>E0 L1>L0")
    kv_near1 = to_second(mid1)
    dq_far1, dx1, dy1 = pairs("far1", 1, [up1, down1], after=[dq_near0])
    rx1, ry1 = to_early(dx1, dy1)
    dq_near1, dz1, far_sum = pairs("near1", 0, [kv_near1], add=[rx0, ry0, rz0], after=[dq_far1])
    rz1 = route(dz1, "E1>E0 L1>L0")
    whole = (2, groups, rows, width)
    dq, dkv = call(
        diag_kernel,
        "diag",
        [SMEM] + [VMEM] * 10,
        [HBM, VMEM],
        [shape(queries.shape, BF16), shape(whole, F32)],
        [pltpu.VMEM(queries.shape, BF16), sem((groups,))],
    )(flags, *rows_in, *parts, dq_near0, dq_near1, dq_far0, dq_far1)
    dk, dv = call(
        final_kernel,
        "final",
        [VMEM] * 5,
        [HBM] * 2,
        [shape(keys.shape, BF16)] * 2,
        [pltpu.VMEM(whole, BF16), sem((2,))],
    )(dkv, far_sum, rx1, ry1, rz1)
    return dq, dk, dv


def solution(mesh):
    spec3 = P(None, AXES, None)
    spec2 = P(None, AXES)
    return jax.shard_map(
        local,
        mesh=mesh,
        in_specs=(spec3, spec3, spec3, spec2, spec3, spec2),
        out_specs=(spec3, spec3, spec3),
        check_vma=False,
    )
```

```python
import functools
import math

import jax
import jax.numpy as jnp
from jax import lax
from jax.experimental import pallas as pl
from jax.experimental.pallas import tpu as pltpu
from jax.sharding import PartitionSpec as P

LOG2E = math.log2(math.e)
NN = (((1,), (0,)), ((), ()))
NT = (((1,), (1,)), ((), ()))
TN = (((0,), (0,)), ((), ()))
AXES = ("ctx", "head")
F32 = jnp.float32
BF16 = jnp.bfloat16
VMEM = pl.BlockSpec(memory_space=pltpu.VMEM)
HBM = pl.BlockSpec(memory_space=pltpu.HBM)
CHUNKS = 2


def dot(a, b, dims):
    return lax.dot_general(a, b, dims, preferred_element_type=F32)


def route(x, pairs):
    far = lax.axis_size("ctx") // 2

    def device(role, c):
        return (c + (far if role[0] == "L" else 0)) * 2 + int(role[1])

    table = []
    for pair in pairs.split():
        src, dst = pair.split(">")
        table += [(device(src, c), device(dst, c)) for c in range(far)]
    return lax.ppermute(x, AXES, table)


def call(kernel, name, in_specs, out_specs, out_shape, scratch=(), aliases=None):
    return pl.pallas_call(
        kernel,
        in_specs=in_specs,
        out_specs=out_specs,
        out_shape=out_shape,
        scratch_shapes=list(scratch),
        input_output_aliases=aliases or {},
        compiler_params=pltpu.CompilerParams(vmem_limit_bytes=24 << 20),
        cost_estimate=pl.CostEstimate(flops=1, bytes_accessed=1 << 20, transcendentals=0),
        name=name,
    )


def group_grads(q_ref, g_ref, lse_ref, delta_ref, g, kvs, at, causal):
    rows, width = q_ref.shape[1:]
    ratio = 8
    lo = g * ratio
    scale = 1.0 / math.sqrt(width)
    q = q_ref[lo : lo + ratio].reshape(ratio * rows, width)
    g_out = g_ref[lo : lo + ratio].reshape(ratio * rows, width)
    base = lo // 16 * 16
    lse = lse_ref[base : base + 16].astype(F32)[lo - base : lo - base + ratio] * LOG2E
    delta = delta_ref[base : base + 16].astype(F32)[lo - base : lo - base + ratio]
    lse_row = jnp.concatenate([lse[i : i + 1, :] for i in range(ratio)], 1)
    delta_row = jnp.concatenate([delta[i : i + 1, :] for i in range(ratio)], 1)
    k = jnp.concatenate([r[0, at] for r in kvs], 0)
    v = jnp.concatenate([r[1, at] for r in kvs], 0)
    probs = jnp.exp2(dot(k, q, NT) * (scale * LOG2E) - lse_row)
    if causal:
        key = lax.broadcasted_iota(jnp.int32, probs.shape, 0)
        row = lax.broadcasted_iota(jnp.int32, probs.shape, 1) % rows
        probs = jnp.where(key <= row, probs, 0.0)
    dprobs = dot(v, g_out, NT)
    dscores = (probs * (dprobs - delta_row)).astype(BF16)
    dvalue = dot(probs.astype(BF16), g_out, NN)
    dkey = dot(dscores, q, NN) * scale
    dquery = dot(dscores, k, TN) * scale
    return dquery.reshape(ratio, rows, width), dkey, dvalue


def pack_kernel(k_ref, v_ref, *refs):
    outs, sem = refs[:-1], refs[-1]
    copies = []
    for i, out in enumerate(outs):
        n = out.shape[1]
        for j, src in enumerate((k_ref, v_ref)):
            copies.append(pltpu.make_async_copy(src.at[pl.ds(i * n, n)], out.at[j], sem.at[2 * i + j]))
    for c in copies:
        c.start()
    for c in copies:
        c.wait()


def repeat(held, later):
    for src, out in zip(held, later):
        out[...] = src[...]


def load_kernel(q_hbm, g_hbm, lse_hbm, delta_hbm, *refs):
    n = (len(refs) - 5) // 2
    held, (q_ref, g_ref, lse_ref, delta_ref), later, sem = (
        refs[:n], refs[n : n + 4], refs[n + 4 : -1], refs[-1]
    )
    copies = [
        pltpu.make_async_copy(lse_hbm, lse_ref, sem.at[0]),
        pltpu.make_async_copy(delta_hbm, delta_ref, sem.at[1]),
    ]
    pieces = 4
    size = q_hbm.shape[0] // pieces
    for i in range(pieces):
        cut = pl.ds(i * size, size)
        copies.append(pltpu.make_async_copy(q_hbm.at[cut], q_ref.at[cut], sem.at[2 + 2 * i]))
        copies.append(pltpu.make_async_copy(g_hbm.at[cut], g_ref.at[cut], sem.at[3 + 2 * i]))
    for c in copies:
        c.start()
    repeat(held, later)
    for c in copies:
        c.wait()


def pair_kernel(first, flag_at, n_kv, n_held, n_after, with_sum, q_ref, g_ref, lse_ref, delta_ref, *refs):
    refs = refs[n_after:]
    if with_sum:
        rx_ref, ry_ref, rz_ref, *refs = refs
        *refs, sum_ref = refs
        sum_ref[...] = rx_ref[...].astype(F32) + ry_ref[...].astype(F32) + rz_ref[...].astype(F32)
    kv_refs, refs = refs[:n_kv], refs[n_kv:]
    held, refs = refs[:n_held], refs[n_held:]
    dq_ref, outs, later = refs[0], refs[1 : 1 + n_kv], refs[1 + n_kv :]
    repeat(held, later)
    groups = kv_refs[0].shape[1]
    rows = q_ref.shape[1]
    ratio = 8

    @pl.when(is_late() if flag_at else is_second())
    def _():
        for i in range(groups):
            dq, dk, dv = group_grads(
                q_ref, g_ref, lse_ref, delta_ref, first + i, kv_refs, i, False
            )
            dq_ref[i * ratio : (i + 1) * ratio] = dq
            for j, out in enumerate(outs):
                out[0, i] = dk[j * rows : (j + 1) * rows].astype(BF16)
                out[1, i] = dv[j * rows : (j + 1) * rows].astype(BF16)


def diag_kernel(q_ref, g_ref, lse_ref, delta_ref, *refs):
    parts, near_refs, far_refs = refs[0:2], refs[2:4], refs[4:6]
    dq_hbm, dkv_ref, dq_half, sem = refs[6:]
    n = parts[0].shape[1]
    ratio = 8
    stores = []
    has_near, has_far = is_second(), is_late()
    for g in range(2 * n):
        c, i = g // n, g % n
        dq, dk, dv = group_grads(q_ref, g_ref, lse_ref, delta_ref, g, [parts[c]], i, True)
        at = slice(g * ratio, (g + 1) * ratio)
        of = slice(i * ratio, (i + 1) * ratio)
        dq = dq + jnp.where(has_near, near_refs[c][of], 0.0)
        dq = dq + jnp.where(has_far, far_refs[c][of], 0.0)
        dq_half[at] = dq.astype(BF16)
        cut = pl.ds(g * ratio, ratio)
        stores.append(pltpu.make_async_copy(dq_half.at[cut], dq_hbm.at[cut], sem.at[g]))
        stores[-1].start()
        dkv_ref[0, g] = dk
        dkv_ref[1, g] = dv
    for c in stores:
        c.wait()


def final_kernel(dkv_ref, sum_ref, rx_ref, ry_ref, rz_ref, dk_hbm, dv_hbm, half, sem):
    n = rz_ref.shape[1]
    copies = []
    for j, out in enumerate((dk_hbm, dv_hbm)):
        half[j, :n] = (dkv_ref[j, :n] + sum_ref[j]).astype(BF16)
        far = rx_ref[j].astype(F32) + ry_ref[j].astype(F32)
        half[j, n:] = (dkv_ref[j, n:] + rz_ref[j].astype(F32) + far).astype(BF16)
        copies.append(pltpu.make_async_copy(half.at[j], out, sem.at[j]))
        copies[-1].start()
    for c in copies:
        c.wait()


def is_second():
    return lax.axis_index("head") == 1


def is_late():
    return lax.axis_index("ctx") >= lax.axis_size("ctx") // 2


def in_hbm(x):
    return pltpu.with_memory_space_constraint(x, pltpu.HBM)


def local(queries, keys, values, delta, grad_out, lse):
    heads, rows, width = queries.shape
    groups = keys.shape[0]
    n = groups // CHUNKS
    shape = jax.ShapeDtypeStruct
    part = shape((2, n, rows, width), BF16)
    dq_part = shape((heads // CHUNKS, rows, width), F32)
    sem = pltpu.SemaphoreType.DMA
    parts = call(
        pack_kernel, "pack", [HBM] * 2, [VMEM] * CHUNKS, [part] * CHUNKS, [sem((2 * CHUNKS,))]
    )(in_hbm(keys), in_hbm(values))

    up0, down0 = route(parts[0], "E0>L0 E1>L1 L0>E0"), route(parts[0], "E0>L1 E1>L0")
    *rows_in, later = call(
        load_kernel,
        "load",
        [HBM] * 4 + [VMEM],
        [VMEM] * 5,
        [shape(x.shape, BF16) for x in (queries, grad_out, lse, delta)] + [part],
        [sem((10,))],
    )(*(in_hbm(x) for x in (queries, grad_out, lse, delta)), parts[1])
    up1, down1 = route(later, "E0>L0 E1>L1 L0>E0"), route(later, "E0>L1 E1>L0")

    def to_second(x):
        return route(x, "E0>L1 L0>E1")

    def to_early(x, y):
        return route(x, "L0>E0 L1>E1"), route(y, "L1>E0 L0>E1")

    def pairs(name, flag_at, kvs, held=(), add=(), after=()):
        n_held, n_sum = len(held), len(add) // 3
        return call(
            functools.partial(
                pair_kernel, int(name[-1]) * n, flag_at, len(kvs), n_held, len(after), n_sum
            ),
            name,
            [VMEM] * (4 + len(after) + len(kvs) + n_held + len(add)),
            [VMEM] * (1 + len(kvs) + n_held + n_sum),
            [dq_part] + [part] * (len(kvs) + n_held) + [shape(part.shape, F32)] * n_sum,
        )(*rows_in, *after, *add, *kvs, *held)

    kv_near0 = to_second(up0)
    dq_far0, dx0, dy0 = pairs("far0", 1, [up0, down0])
    rx0, ry0 = to_early(dx0, dy0)
    dq_near0, dz0, mid1 = pairs("near0", 0, [kv_near0], held=[up1], after=[dq_far0])
    rz0 = route(dz0, "E1>E0 L1>L0")
    kv_near1 = to_second(mid1)
    dq_far1, dx1, dy1 = pairs("far1", 1, [up1, down1], after=[dq_near0])
    rx1, ry1 = to_early(dx1, dy1)
    dq_near1, dz1, far_sum = pairs("near1", 0, [kv_near1], add=[rx0, ry0, rz0], after=[dq_far1])
    rz1 = route(dz1, "E1>E0 L1>L0")
    whole = (2, groups, rows, width)
    dq, dkv = call(
        diag_kernel,
        "diag",
        [VMEM] * 10,
        [HBM, VMEM],
        [shape(queries.shape, BF16), shape(whole, F32)],
        [pltpu.VMEM(queries.shape, BF16), sem((groups,))],
    )(*rows_in, *parts, dq_near0, dq_near1, dq_far0, dq_far1)
    dk, dv = call(
        final_kernel,
        "final",
        [VMEM] * 5,
        [HBM] * 2,
        [shape(keys.shape, BF16)] * 2,
        [pltpu.VMEM(whole, BF16), sem((2,))],
    )(dkv, far_sum, rx1, ry1, rz1)
    return dq, dk, dv


def solution(mesh):
    spec3 = P(None, AXES, None)
    spec2 = P(None, AXES)
    return jax.shard_map(
        local,
        mesh=mesh,
        in_specs=(spec3, spec3, spec3, spec2, spec3, spec2),
        out_specs=(spec3, spec3, spec3),
        check_vma=False,
    )
```

```python
import functools
import math

import jax
import jax.numpy as jnp
from jax import lax
from jax.experimental import pallas as pl
from jax.experimental.pallas import tpu as pltpu
from jax.sharding import PartitionSpec as P

LOG2E = math.log2(math.e)
NN = (((1,), (0,)), ((), ()))
NT = (((1,), (1,)), ((), ()))
TN = (((0,), (0,)), ((), ()))
AXES = ("ctx", "head")
F32 = jnp.float32
BF16 = jnp.bfloat16
VMEM = pl.BlockSpec(memory_space=pltpu.VMEM)
HBM = pl.BlockSpec(memory_space=pltpu.HBM)
CHUNKS = 2


def dot(a, b, dims):
    return lax.dot_general(a, b, dims, preferred_element_type=F32)


def route(x, pairs):
    far = lax.axis_size("ctx") // 2

    def device(role, c):
        return (c + (far if role[0] == "L" else 0)) * 2 + int(role[1])

    table = []
    for pair in pairs.split():
        src, dst = pair.split(">")
        table += [(device(src, c), device(dst, c)) for c in range(far)]
    return lax.ppermute(x, AXES, table)


def call(kernel, name, in_specs, out_specs, out_shape, scratch=(), aliases=None):
    return pl.pallas_call(
        kernel,
        in_specs=in_specs,
        out_specs=out_specs,
        out_shape=out_shape,
        scratch_shapes=list(scratch),
        input_output_aliases=aliases or {},
        compiler_params=pltpu.CompilerParams(vmem_limit_bytes=24 << 20),
        cost_estimate=pl.CostEstimate(flops=1, bytes_accessed=1 << 20, transcendentals=0),
        name=name,
    )


def group_grads(q_ref, g_ref, lse_ref, delta_ref, g, kvs, at, causal):
    rows, width = q_ref.shape[1:]
    ratio = 8
    lo = g * ratio
    scale = 1.0 / math.sqrt(width)
    q = q_ref[lo : lo + ratio].reshape(ratio * rows, width)
    g_out = g_ref[lo : lo + ratio].reshape(ratio * rows, width)
    base = lo // 16 * 16
    lse = lse_ref[base : base + 16].astype(F32)[lo - base : lo - base + ratio] * LOG2E
    delta = delta_ref[base : base + 16].astype(F32)[lo - base : lo - base + ratio]
    lse_row = jnp.concatenate([lse[i : i + 1, :] for i in range(ratio)], 1)
    delta_row = jnp.concatenate([delta[i : i + 1, :] for i in range(ratio)], 1)
    k = jnp.concatenate([r[0, at] for r in kvs], 0)
    v = jnp.concatenate([r[1, at] for r in kvs], 0)
    probs = jnp.exp2(dot(k, q, NT) * (scale * LOG2E) - lse_row)
    if causal:
        key = lax.broadcasted_iota(jnp.int32, probs.shape, 0)
        row = lax.broadcasted_iota(jnp.int32, probs.shape, 1) % rows
        probs = jnp.where(key <= row, probs, 0.0)
    dprobs = dot(v, g_out, NT)
    dscores = (probs * (dprobs - delta_row)).astype(BF16)
    dvalue = dot(probs.astype(BF16), g_out, NN)
    dkey = dot(dscores, q, NN) * scale
    dquery = dot(dscores, k, TN) * scale
    return dquery.reshape(ratio, rows, width), dkey, dvalue


def pack_kernel(k_ref, v_ref, *refs):
    sources, outs, rows_refs, sem, rows_sem = refs[:4], refs[4:-6], refs[-6:-2], refs[-2], refs[-1]
    copies = []
    for i, out in enumerate(outs):
        n = out.shape[1]
        for j, src in enumerate((k_ref, v_ref)):
            copies.append(pltpu.make_async_copy(src.at[pl.ds(i * n, n)], out.at[j], sem.at[2 * i + j]))
    for c in copies:
        c.start()

    @pl.when(loads_first())
    def _():
        load_rows(sources, rows_refs, rows_sem)

    for c in copies:
        c.wait()


def repeat(held, later):
    for src, out in zip(held, later):
        out[...] = src[...]


def load_rows(sources, targets, sem):
    (q_hbm, g_hbm, lse_hbm, delta_hbm), (q_ref, g_ref, lse_ref, delta_ref) = sources, targets
    copies = [
        pltpu.make_async_copy(lse_hbm, lse_ref, sem.at[0]),
        pltpu.make_async_copy(delta_hbm, delta_ref, sem.at[1]),
    ]
    pieces = 4
    size = q_hbm.shape[0] // pieces
    for i in range(pieces):
        cut = pl.ds(i * size, size)
        copies.append(pltpu.make_async_copy(q_hbm.at[cut], q_ref.at[cut], sem.at[2 + 2 * i]))
        copies.append(pltpu.make_async_copy(g_hbm.at[cut], g_ref.at[cut], sem.at[3 + 2 * i]))
    for c in copies:
        c.start()
    for c in copies:
        c.wait()


def load_kernel(*refs):
    sources, held, rows_refs, later, sem = refs[:4], refs[8], refs[9:13], refs[13], refs[14]
    later[...] = held[...]

    @pl.when(jnp.logical_not(loads_first()))
    def _():
        load_rows(sources, rows_refs, sem)


def pair_kernel(first, flag_at, n_kv, n_held, n_after, with_sum, q_ref, g_ref, lse_ref, delta_ref, *refs):
    refs = refs[n_after:]
    if with_sum:
        rx_ref, ry_ref, rz_ref, *refs = refs
        *refs, sum_ref = refs
        sum_ref[...] = rx_ref[...].astype(F32) + ry_ref[...].astype(F32) + rz_ref[...].astype(F32)
    kv_refs, refs = refs[:n_kv], refs[n_kv:]
    held, refs = refs[:n_held], refs[n_held:]
    dq_ref, outs, later = refs[0], refs[1 : 1 + n_kv], refs[1 + n_kv :]
    repeat(held, later)
    groups = kv_refs[0].shape[1]
    rows = q_ref.shape[1]
    ratio = 8

    @pl.when(is_late() if flag_at else is_second())
    def _():
        for i in range(groups):
            dq, dk, dv = group_grads(
                q_ref, g_ref, lse_ref, delta_ref, first + i, kv_refs, i, False
            )
            dq_ref[i * ratio : (i + 1) * ratio] = dq
            for j, out in enumerate(outs):
                out[0, i] = dk[j * rows : (j + 1) * rows].astype(BF16)
                out[1, i] = dv[j * rows : (j + 1) * rows].astype(BF16)


def diag_kernel(q_ref, g_ref, lse_ref, delta_ref, *refs):
    parts, near_refs, far_refs = refs[0:2], refs[2:4], refs[4:6]
    dq_hbm, dkv_ref, dq_half, sem = refs[6:]
    n = parts[0].shape[1]
    ratio = 8
    stores = []
    has_near, has_far = is_second(), is_late()
    for g in range(2 * n):
        c, i = g // n, g % n
        dq, dk, dv = group_grads(q_ref, g_ref, lse_ref, delta_ref, g, [parts[c]], i, True)
        at = slice(g * ratio, (g + 1) * ratio)
        of = slice(i * ratio, (i + 1) * ratio)
        dq = dq + jnp.where(has_near, near_refs[c][of], 0.0)
        dq = dq + jnp.where(has_far, far_refs[c][of], 0.0)
        dq_half[at] = dq.astype(BF16)
        cut = pl.ds(g * ratio, ratio)
        stores.append(pltpu.make_async_copy(dq_half.at[cut], dq_hbm.at[cut], sem.at[g]))
        stores[-1].start()
        dkv_ref[0, g] = dk
        dkv_ref[1, g] = dv
    for c in stores:
        c.wait()


def final_kernel(dkv_ref, sum_ref, rx_ref, ry_ref, rz_ref, dk_hbm, dv_hbm, half, sem):
    n = rz_ref.shape[1]
    copies = []
    for j, out in enumerate((dk_hbm, dv_hbm)):
        half[j, :n] = (dkv_ref[j, :n] + sum_ref[j]).astype(BF16)
        far = rx_ref[j].astype(F32) + ry_ref[j].astype(F32)
        half[j, n:] = (dkv_ref[j, n:] + rz_ref[j].astype(F32) + far).astype(BF16)
        copies.append(pltpu.make_async_copy(half.at[j], out, sem.at[j]))
        copies[-1].start()
    for c in copies:
        c.wait()


def is_second():
    return lax.axis_index("head") == 1


def is_late():
    return lax.axis_index("ctx") >= lax.axis_size("ctx") // 2


def loads_first():
    return lax.rem(lax.axis_index("ctx"), 2) == 0


def in_hbm(x):
    return pltpu.with_memory_space_constraint(x, pltpu.HBM)


def local(queries, keys, values, delta, grad_out, lse):
    heads, rows, width = queries.shape
    groups = keys.shape[0]
    n = groups // CHUNKS
    shape = jax.ShapeDtypeStruct
    part = shape((2, n, rows, width), BF16)
    dq_part = shape((heads // CHUNKS, rows, width), F32)
    sem = pltpu.SemaphoreType.DMA
    rows_hbm = [in_hbm(x) for x in (queries, grad_out, lse, delta)]
    rows_shape = [shape(x.shape, BF16) for x in rows_hbm]
    *parts, r0, r1, r2, r3 = call(
        pack_kernel,
        "pack",
        [HBM] * 6,
        [VMEM] * (CHUNKS + 4),
        [part] * CHUNKS + rows_shape,
        [sem((2 * CHUNKS,)), sem((10,))],
    )(in_hbm(keys), in_hbm(values), *rows_hbm)

    up0, down0 = route(parts[0], "E0>L0 E1>L1 L0>E0"), route(parts[0], "E0>L1 E1>L0")
    *rows_in, later = call(
        load_kernel,
        "load",
        [HBM] * 4 + [VMEM] * 5,
        [VMEM] * 5,
        rows_shape + [part],
        [sem((10,))],
        {4: 0, 5: 1, 6: 2, 7: 3},
    )(*rows_hbm, r0, r1, r2, r3, parts[1])
    up1, down1 = route(later, "E0>L0 E1>L1 L0>E0"), route(later, "E0>L1 E1>L0")

    def to_second(x):
        return route(x, "E0>L1 L0>E1")

    def to_early(x, y):
        return route(x, "L0>E0 L1>E1"), route(y, "L1>E0 L0>E1")

    def pairs(name, flag_at, kvs, held=(), add=(), after=()):
        n_held, n_sum = len(held), len(add) // 3
        return call(
            functools.partial(
                pair_kernel, int(name[-1]) * n, flag_at, len(kvs), n_held, len(after), n_sum
            ),
            name,
            [VMEM] * (4 + len(after) + len(kvs) + n_held + len(add)),
            [VMEM] * (1 + len(kvs) + n_held + n_sum),
            [dq_part] + [part] * (len(kvs) + n_held) + [shape(part.shape, F32)] * n_sum,
        )(*rows_in, *after, *add, *kvs, *held)

    kv_near0 = to_second(up0)
    dq_far0, dx0, dy0 = pairs("far0", 1, [up0, down0])
    rx0, ry0 = to_early(dx0, dy0)
    dq_near0, dz0, mid1 = pairs("near0", 0, [kv_near0], held=[up1], after=[dq_far0])
    rz0 = route(dz0, "E1>E0 L1>L0")
    kv_near1 = to_second(mid1)
    dq_far1, dx1, dy1 = pairs("far1", 1, [up1, down1], after=[dq_near0])
    rx1, ry1 = to_early(dx1, dy1)
    dq_near1, dz1, far_sum = pairs("near1", 0, [kv_near1], add=[rx0, ry0, rz0], after=[dq_far1])
    rz1 = route(dz1, "E1>E0 L1>L0")
    whole = (2, groups, rows, width)
    dq, dkv = call(
        diag_kernel,
        "diag",
        [VMEM] * 10,
        [HBM, VMEM],
        [shape(queries.shape, BF16), shape(whole, F32)],
        [pltpu.VMEM(queries.shape, BF16), sem((groups,))],
    )(*rows_in, *parts, dq_near0, dq_near1, dq_far0, dq_far1)
    dk, dv = call(
        final_kernel,
        "final",
        [VMEM] * 5,
        [HBM] * 2,
        [shape(keys.shape, BF16)] * 2,
        [pltpu.VMEM(whole, BF16), sem((2,))],
    )(dkv, far_sum, rx1, ry1, rz1)
    return dq, dk, dv


def solution(mesh):
    spec3 = P(None, AXES, None)
    spec2 = P(None, AXES)
    return jax.shard_map(
        local,
        mesh=mesh,
        in_specs=(spec3, spec3, spec3, spec2, spec3, spec2),
        out_specs=(spec3, spec3, spec3),
        check_vma=False,
    )
```

```python
import functools
import math

import jax
import jax.numpy as jnp
from jax import lax
from jax.experimental import pallas as pl
from jax.experimental.pallas import tpu as pltpu
from jax.sharding import PartitionSpec as P

LOG2E = math.log2(math.e)
NN = (((1,), (0,)), ((), ()))
NT = (((1,), (1,)), ((), ()))
TN = (((0,), (0,)), ((), ()))
AXES = ("ctx", "head")
F32 = jnp.float32
BF16 = jnp.bfloat16
VMEM = pl.BlockSpec(memory_space=pltpu.VMEM)
HBM = pl.BlockSpec(memory_space=pltpu.HBM)
CHUNKS = 2


def dot(a, b, dims):
    return lax.dot_general(a, b, dims, preferred_element_type=F32)


def route(x, pairs):
    far = lax.axis_size("ctx") // 2

    def device(role, c):
        return (c + (far if role[0] == "L" else 0)) * 2 + int(role[1])

    table = []
    for pair in pairs.split():
        src, dst = pair.split(">")
        table += [(device(src, c), device(dst, c)) for c in range(far)]
    return lax.ppermute(x, AXES, table)


def call(kernel, name, in_specs, out_specs, out_shape, scratch=(), aliases=None):
    return pl.pallas_call(
        kernel,
        in_specs=in_specs,
        out_specs=out_specs,
        out_shape=out_shape,
        scratch_shapes=list(scratch),
        input_output_aliases=aliases or {},
        compiler_params=pltpu.CompilerParams(vmem_limit_bytes=24 << 20),
        cost_estimate=pl.CostEstimate(flops=1, bytes_accessed=1 << 20, transcendentals=0),
        name=name,
    )


def group_grads(q_ref, g_ref, lse_ref, delta_ref, g, kvs, at, causal):
    rows, width = q_ref.shape[1:]
    ratio = 8
    lo = g * ratio
    scale = 1.0 / math.sqrt(width)
    q = q_ref[lo : lo + ratio].reshape(ratio * rows, width)
    g_out = g_ref[lo : lo + ratio].reshape(ratio * rows, width)
    base = lo // 16 * 16
    lse = lse_ref[base : base + 16].astype(F32)[lo - base : lo - base + ratio] * LOG2E
    delta = delta_ref[base : base + 16].astype(F32)[lo - base : lo - base + ratio]
    lse_row = jnp.concatenate([lse[i : i + 1, :] for i in range(ratio)], 1)
    delta_row = jnp.concatenate([delta[i : i + 1, :] for i in range(ratio)], 1)
    k = jnp.concatenate([r[0, at] for r in kvs], 0)
    v = jnp.concatenate([r[1, at] for r in kvs], 0)
    probs = jnp.exp2(dot(k, q, NT) * (scale * LOG2E) - lse_row)
    if causal:
        key = lax.broadcasted_iota(jnp.int32, probs.shape, 0)
        row = lax.broadcasted_iota(jnp.int32, probs.shape, 1) % rows
        probs = jnp.where(key <= row, probs, 0.0)
    dprobs = dot(v, g_out, NT)
    dscores = (probs * (dprobs - delta_row)).astype(BF16)
    dvalue = dot(probs.astype(BF16), g_out, NN)
    dkey = dot(dscores, q, NN) * scale
    dquery = dot(dscores, k, TN) * scale
    return dquery.reshape(ratio, rows, width), dkey, dvalue


def pack_kernel(k_ref, v_ref, *refs):
    sources, outs, rows_refs, sem, rows_sem = refs[:4], refs[4:-6], refs[-6:-2], refs[-2], refs[-1]
    copies = []
    for i, out in enumerate(outs):
        n = out.shape[1]
        for j, src in enumerate((k_ref, v_ref)):
            copies.append(pltpu.make_async_copy(src.at[pl.ds(i * n, n)], out.at[j], sem.at[2 * i + j]))
    for c in copies:
        c.start()

    @pl.when(loads_first())
    def _():
        load_rows(sources, rows_refs, rows_sem)

    for c in copies:
        c.wait()


def repeat(held, later):
    for src, out in zip(held, later):
        out[...] = src[...]


def load_rows(sources, targets, sem):
    (q_hbm, g_hbm, lse_hbm, delta_hbm), (q_ref, g_ref, lse_ref, delta_ref) = sources, targets
    copies = [
        pltpu.make_async_copy(lse_hbm, lse_ref, sem.at[0]),
        pltpu.make_async_copy(delta_hbm, delta_ref, sem.at[1]),
    ]
    pieces = 4
    size = q_hbm.shape[0] // pieces
    for i in range(pieces):
        cut = pl.ds(i * size, size)
        copies.append(pltpu.make_async_copy(q_hbm.at[cut], q_ref.at[cut], sem.at[2 + 2 * i]))
        copies.append(pltpu.make_async_copy(g_hbm.at[cut], g_ref.at[cut], sem.at[3 + 2 * i]))
    for c in copies:
        c.start()
    for c in copies:
        c.wait()


def load_kernel(*refs):
    sources, held, rows_refs, later, sem = refs[:4], refs[8], refs[9:13], refs[13], refs[14]
    later[...] = held[...]

    @pl.when(jnp.logical_not(loads_first()))
    def _():
        load_rows(sources, rows_refs, sem)


def pair_kernel(first, flag_at, n_kv, n_held, n_after, with_sum, q_ref, g_ref, lse_ref, delta_ref, *refs):
    refs = refs[n_after:]
    if with_sum:
        rx_ref, ry_ref, rz_ref, *refs = refs
        *refs, sum_ref = refs
        sum_ref[...] = rx_ref[...].astype(F32) + ry_ref[...].astype(F32) + rz_ref[...].astype(F32)
    kv_refs, refs = refs[:n_kv], refs[n_kv:]
    held, refs = refs[:n_held], refs[n_held:]
    dq_ref, outs, later = refs[0], refs[1 : 1 + n_kv], refs[1 + n_kv :]
    repeat(held, later)
    groups = kv_refs[0].shape[1]
    rows = q_ref.shape[1]
    ratio = 8

    @pl.when(is_late() if flag_at else is_second())
    def _():
        for i in range(groups):
            dq, dk, dv = group_grads(
                q_ref, g_ref, lse_ref, delta_ref, first + i, kv_refs, i, False
            )
            dq_ref[i * ratio : (i + 1) * ratio] = dq
            for j, out in enumerate(outs):
                out[0, i] = dk[j * rows : (j + 1) * rows].astype(BF16)
                out[1, i] = dv[j * rows : (j + 1) * rows].astype(BF16)


def diag_kernel(q_ref, g_ref, lse_ref, delta_ref, *refs):
    parts, near_refs, far_refs = refs[0:2], refs[2:4], refs[4:6]
    far_sum, dq_hbm, dk_hbm, dv_hbm, dkv_ref, dq_half, half, sem, kv_sem = refs[6:]
    n = parts[0].shape[1]
    ratio = 8
    stores = []
    has_near, has_far = is_second(), is_late()
    for g in range(2 * n):
        c, i = g // n, g % n
        dq, dk, dv = group_grads(q_ref, g_ref, lse_ref, delta_ref, g, [parts[c]], i, True)
        at = slice(g * ratio, (g + 1) * ratio)
        of = slice(i * ratio, (i + 1) * ratio)
        dq = dq + jnp.where(has_near, near_refs[c][of], 0.0)
        dq = dq + jnp.where(has_far, far_refs[c][of], 0.0)
        dq_half[at] = dq.astype(BF16)
        cut = pl.ds(g * ratio, ratio)
        stores.append(pltpu.make_async_copy(dq_half.at[cut], dq_hbm.at[cut], sem.at[g]))
        stores[-1].start()
        if c:
            dkv_ref[0, i] = dk
            dkv_ref[1, i] = dv
        else:
            half[0, i] = (dk + far_sum[0, i]).astype(BF16)
            half[1, i] = (dv + far_sum[1, i]).astype(BF16)
        if g == n - 1:
            for j, out in enumerate((dk_hbm, dv_hbm)):
                stores.append(
                    pltpu.make_async_copy(half.at[j], out.at[pl.ds(0, n)], kv_sem.at[j])
                )
                stores[-1].start()
    for c in stores:
        c.wait()


def final_kernel(dkv_ref, rx_ref, ry_ref, rz_ref, *refs):
    dk_hbm, dv_hbm, half, sem = refs[-4:]
    n = rz_ref.shape[1]
    copies = []
    for j, out in enumerate((dk_hbm, dv_hbm)):
        far = rx_ref[j].astype(F32) + ry_ref[j].astype(F32)
        half[j] = (dkv_ref[j] + rz_ref[j].astype(F32) + far).astype(BF16)
        copies.append(pltpu.make_async_copy(half.at[j], out.at[pl.ds(n, n)], sem.at[j]))
        copies[-1].start()
    for c in copies:
        c.wait()


def is_second():
    return lax.axis_index("head") == 1


def is_late():
    return lax.axis_index("ctx") >= lax.axis_size("ctx") // 2


def loads_first():
    return lax.rem(lax.axis_index("ctx"), 2) == 0


def in_hbm(x):
    return pltpu.with_memory_space_constraint(x, pltpu.HBM)


def local(queries, keys, values, delta, grad_out, lse):
    heads, rows, width = queries.shape
    groups = keys.shape[0]
    n = groups // CHUNKS
    shape = jax.ShapeDtypeStruct
    part = shape((2, n, rows, width), BF16)
    dq_part = shape((heads // CHUNKS, rows, width), F32)
    sem = pltpu.SemaphoreType.DMA
    rows_hbm = [in_hbm(x) for x in (queries, grad_out, lse, delta)]
    rows_shape = [shape(x.shape, BF16) for x in rows_hbm]
    *parts, r0, r1, r2, r3 = call(
        pack_kernel,
        "pack",
        [HBM] * 6,
        [VMEM] * (CHUNKS + 4),
        [part] * CHUNKS + rows_shape,
        [sem((2 * CHUNKS,)), sem((10,))],
    )(in_hbm(keys), in_hbm(values), *rows_hbm)

    up0, down0 = route(parts[0], "E0>L0 E1>L1 L0>E0"), route(parts[0], "E0>L1 E1>L0")
    *rows_in, later = call(
        load_kernel,
        "load",
        [HBM] * 4 + [VMEM] * 5,
        [VMEM] * 5,
        rows_shape + [part],
        [sem((10,))],
        {4: 0, 5: 1, 6: 2, 7: 3},
    )(*rows_hbm, r0, r1, r2, r3, parts[1])
    up1, down1 = route(later, "E0>L0 E1>L1 L0>E0"), route(later, "E0>L1 E1>L0")

    def to_second(x):
        return route(x, "E0>L1 L0>E1")

    def to_early(x, y):
        return route(x, "L0>E0 L1>E1"), route(y, "L1>E0 L0>E1")

    def pairs(name, flag_at, kvs, held=(), add=(), after=()):
        n_held, n_sum = len(held), len(add) // 3
        return call(
            functools.partial(
                pair_kernel, int(name[-1]) * n, flag_at, len(kvs), n_held, len(after), n_sum
            ),
            name,
            [VMEM] * (4 + len(after) + len(kvs) + n_held + len(add)),
            [VMEM] * (1 + len(kvs) + n_held + n_sum),
            [dq_part] + [part] * (len(kvs) + n_held) + [shape(part.shape, F32)] * n_sum,
        )(*rows_in, *after, *add, *kvs, *held)

    kv_near0 = to_second(up0)
    dq_far0, dx0, dy0 = pairs("far0", 1, [up0, down0])
    rx0, ry0 = to_early(dx0, dy0)
    dq_near0, dz0, mid1 = pairs("near0", 0, [kv_near0], held=[up1], after=[dq_far0])
    rz0 = route(dz0, "E1>E0 L1>L0")
    kv_near1 = to_second(mid1)
    dq_far1, dx1, dy1 = pairs("far1", 1, [up1, down1], after=[dq_near0])
    rx1, ry1 = to_early(dx1, dy1)
    dq_near1, dz1, far_sum = pairs("near1", 0, [kv_near1], add=[rx0, ry0, rz0], after=[dq_far1])
    rz1 = route(dz1, "E1>E0 L1>L0")
    whole = shape(keys.shape, BF16)
    dq, dk, dv, dkv = call(
        diag_kernel,
        "diag",
        [VMEM] * 11,
        [HBM] * 3 + [VMEM],
        [shape(queries.shape, BF16), whole, whole, shape(part.shape, F32)],
        [
            pltpu.VMEM(queries.shape, BF16),
            pltpu.VMEM(part.shape, BF16),
            sem((groups,)),
            sem((2,)),
        ],
    )(*rows_in, *parts, dq_near0, dq_near1, dq_far0, dq_far1, far_sum)
    dk, dv = call(
        final_kernel,
        "final",
        [VMEM] * 4 + [HBM] * 2,
        [HBM] * 2,
        [whole] * 2,
        [pltpu.VMEM(part.shape, BF16), sem((2,))],
        {4: 0, 5: 1},
    )(dkv, rx1, ry1, rz1, dk, dv)
    return dq, dk, dv


def solution(mesh):
    spec3 = P(None, AXES, None)
    spec2 = P(None, AXES)
    return jax.shard_map(
        local,
        mesh=mesh,
        in_specs=(spec3, spec3, spec3, spec2, spec3, spec2),
        out_specs=(spec3, spec3, spec3),
        check_vma=False,
    )
```
